32 devices in a mesh: rows: 8 (over y, x, core), cols: 4 (over z).
Axes of the slice: x: 2, y: 2, z: 4, core: 2. Of those that a mesh axis runs over, the one named last changes fastest.
Arguments:
- generator: bfloat16 [2048, 64, 448], P('rows'), may hold values from -0.25 to 0.25
- listed_block_columns: int32 [2048, 7], P('rows'), may hold values from -1 to 2047, as said below
- basis: bfloat16 [131072, 1024], P('rows', 'cols'), may hold values from -0.31445312 to 0.31445312
Outputs:
- projected: float32 [1024, 1024], P('rows', 'cols')
The draws below stay inside these ranges and needn't reach their ends.
Inputs may be any that keep to these rules, and one draw needn't show every extreme that they name: `listed_block_columns`: entry 0 of each list is its own block-row index i; every other entry is -1 or a block-row index within 128 of i; entries 5 and 6 are i - 128 and i + 128 wherever these lie in 0 to 2047, else -1.
All inputs are finite; a program needn't handle non-finite values.
Results may differ from the reference program's by a relative error of at most 0.0029.
Values may be sent and summed in bfloat16 or wider, within the bound.
A program may use at most 256 MiB of HBM per device.

```python
import jax
import jax.numpy as jnp
from jax import lax

BLOCK_STATES = 64
LISTED_PER_ROW = 7
K = 1024
BLOCK_ROWS_LOCAL = 256
TOTAL_BLOCK_ROWS = 2048
NSTATES = 131072
FAR = 128


def draw_listed_block_columns(key, part):
    first_key = jax.random.fold_in(key, 11)
    secondary_random_key = jax.random.fold_in(key, 23)
    own = jnp.arange(TOTAL_BLOCK_ROWS, dtype=jnp.int32)[:, None]
    middle = jax.random.randint(first_key, (TOTAL_BLOCK_ROWS, 1), 2, FAR + 1).astype(jnp.int32)
    ones = jnp.ones((TOTAL_BLOCK_ROWS, 1), jnp.int32)
    offsets = jnp.concatenate([0 * ones, -ones, ones, -middle, middle, -FAR * ones, FAR * ones], axis=1)
    columns = own + offsets
    random_samples = jax.random.randint(secondary_random_key, (TOTAL_BLOCK_ROWS, LISTED_PER_ROW), 0, 8)
    listing_index = jnp.arange(LISTED_PER_ROW, dtype=jnp.int32)[None, :]
    keep = (random_samples > 0) | (listing_index == 0) | (listing_index >= 5)
    valid = (columns >= 0) & (columns < TOTAL_BLOCK_ROWS) & keep
    return jnp.where(valid, columns, -1).astype(jnp.int32)


def spiked(entries, rng, source, target, shards_of, factor):
    def block_of(axis_at):
        return (jnp.arange(entries.shape[axis_at]) // (entries.shape[axis_at] // shards_of)).reshape((-1,) + (1,) * (entries.ndim - 1 - axis_at))

    near = jax.random.permutation(rng, shards_of)[block_of(target)]
    other_side = (block_of(target) + shards_of // 2) % shards_of
    return jnp.where((block_of(source) == near) | (block_of(source) == other_side), factor * entries, entries)


def level_of(key, shape, pieces, smallest, largest):
    gain, own = 1.0, jax.random.fold_in(key, 6)
    for dim, blocks in pieces:
        steps = jnp.exp(jax.random.uniform(jax.random.fold_in(own, dim), (blocks,), jnp.float32, smallest / len(pieces), largest / len(pieces)))
        gain = gain * jnp.repeat(steps, shape[dim] // blocks).reshape([-1 if axis == dim else 1 for axis in range(len(shape))])
    return gain


def bell_draw(rng, shape, scale, most, cuts=(), held_as=jnp.bfloat16):
    result = scale * jax.random.normal(rng, shape, jnp.float32)
    if cuts:
        result = result * level_of(rng, shape, cuts, -0.22, 0.18)
    return jnp.clip(result, -most, most).astype(held_as)


def noise_with(rng, dims, scale, bound, split, heavy, kind=jnp.bfloat16):
    entries = scale * jax.random.normal(rng, dims, jnp.float32)
    if split:
        entries = entries * level_of(rng, dims, split, -0.22, 0.18)
    return jnp.clip(spiked(entries, jax.random.fold_in(rng, 3), *heavy), -bound, bound).astype(kind)


def setup_inputs(seed: int = 0) -> dict:
    key_of = jax.random.split(jax.random.key(seed), 4)
    return {
        "generator": bell_draw(key_of[0], (TOTAL_BLOCK_ROWS, BLOCK_STATES, LISTED_PER_ROW * BLOCK_STATES), (LISTED_PER_ROW * BLOCK_STATES) ** -0.5, 0.25, ((0, 8),)),
        "listed_block_columns": draw_listed_block_columns(jax.random.fold_in(key_of[3], 71), 0),
        "basis": noise_with(key_of[2], (NSTATES, K), (NSTATES ** -0.25), 0.31445312, ((0, 8), (1, 4)), (0, 1, 8, 2.0)),
    }


def reference(generator, listed_block_columns, basis):
    nblk = listed_block_columns.shape[0]
    basis_width = basis.shape[1]
    blocks = basis.reshape(nblk, BLOCK_STATES, basis_width)

    def apply_block_group(pair):
        strip, column_indices = pair
        valid = column_indices >= 0
        safe = jnp.where(valid, column_indices, 0).astype(jnp.int32)
        selected_columns = blocks[safe]
        selected_columns = jnp.where(valid[:, :, None, None], selected_columns, jnp.zeros((), basis.dtype))
        selected_columns = selected_columns.reshape(column_indices.shape[0], LISTED_PER_ROW * BLOCK_STATES, basis_width)
        total = jnp.einsum('gik,gkn->gin', strip.astype(jnp.float32), selected_columns.astype(jnp.float32))
        return total.astype(jnp.bfloat16)

    block_groupings = nblk // BLOCK_ROWS_LOCAL
    operator_output = lax.map(apply_block_group, (generator.reshape(block_groupings, BLOCK_ROWS_LOCAL, BLOCK_STATES, LISTED_PER_ROW * BLOCK_STATES), listed_block_columns.reshape(block_groupings, BLOCK_ROWS_LOCAL, LISTED_PER_ROW)))
    operator_output = operator_output.reshape(nblk * BLOCK_STATES, basis_width)
    return lax.dot_general(basis, operator_output, (((0,), (0,)), ((), ())), preferred_element_type=jnp.float32)
```

```python
import functools

import jax
import jax.numpy as jnp
from jax import lax
from jax.experimental import pallas as pl
from jax.experimental.pallas import tpu as pltpu
from jax.sharding import PartitionSpec as P

VMEM_LIMIT = 56 * 1024 * 1024


def apply_kernel(index, before, own, after, generator, applied, stacks, sems, *, bsize, slots, group):
    step = pl.program_id(0)
    low, mid = before.shape[0], own.shape[0]
    high = after.shape[0]

    @pl.when(step == 0)
    def _():
        copies = [
            pltpu.make_async_copy(before, stacks.at[pl.ds(0, low)], sems.at[0]),
            pltpu.make_async_copy(own, stacks.at[pl.ds(low, mid)], sems.at[1]),
            pltpu.make_async_copy(after, stacks.at[pl.ds(low + mid, high)], sems.at[2]),
        ]
        for copy in copies:
            copy.start()
        stacks[pl.ds(low + mid + high, bsize), :] = jnp.zeros((bsize, own.shape[1]), own.dtype)
        for copy in copies:
            copy.wait()

    for g in range(group):
        base = (step * group + g) * slots
        blocks = [
            stacks[pl.ds(pl.multiple_of(index[base + s] * bsize, bsize), bsize), :] for s in range(slots)
        ]
        total = jnp.dot(generator[g], jnp.concatenate(blocks, axis=0), preferred_element_type=jnp.float32)
        applied[g * bsize : (g + 1) * bsize, :] = total.astype(applied.dtype)


def apply_blocks(index, before, own, after, generator):
    brows, bsize, width = generator.shape
    slots = width // bsize
    panel = own.shape[1]
    group = 16
    rows = before.shape[0] + own.shape[0] + after.shape[0] + bsize
    anywhere = pl.BlockSpec(memory_space=pl.ANY)
    return pl.pallas_call(
        functools.partial(apply_kernel, bsize=bsize, slots=slots, group=group),
        grid_spec=pltpu.PrefetchScalarGridSpec(
            num_scalar_prefetch=1,
            grid=(brows // group,),
            in_specs=[anywhere, anywhere, anywhere, pl.BlockSpec((group, bsize, width), lambda i, index: (i, 0, 0))],
            out_specs=pl.BlockSpec((group * bsize, panel), lambda i, index: (i, 0)),
            scratch_shapes=[pltpu.VMEM((rows, panel), own.dtype), pltpu.SemaphoreType.DMA((3,))],
        ),
        out_shape=jax.ShapeDtypeStruct(own.shape, own.dtype),
        compiler_params=pltpu.CompilerParams(vmem_limit_bytes=VMEM_LIMIT),
        cost_estimate=pl.CostEstimate(
            flops=2 * brows * bsize * width * panel, bytes_accessed=48 * 1024 * 1024, transcendentals=0
        ),
    )(index, before, own, after, generator)


def product_kernel(left, right, out, total):
    step = pl.program_id(0)
    panels = left.shape[0]

    @pl.when(step == 0)
    def _():
        total[...] = jnp.zeros_like(total)

    rights = jnp.concatenate([right[c] for c in range(right.shape[0])], axis=1)
    panel = left.shape[2]
    for c in range(panels):
        total[c * panel : (c + 1) * panel, :] += lax.dot_general(
            left[c], rights, (((0,), (0,)), ((), ())), preferred_element_type=jnp.float32
        )

    @pl.when(step == pl.num_programs(0) - 1)
    def _():
        height, width = out.shape[2], out.shape[3]
        for r in range(out.shape[0]):
            for c in range(out.shape[1]):
                out[r, c] = total[r * height : (r + 1) * height, c * width : (c + 1) * width].astype(out.dtype)


def product(left, right, row_count, col_count):
    panels, depth, panel = left.shape
    width = panels * panel
    tile = 512
    spec = pl.BlockSpec((panels, tile, panel), lambda i: (0, i, 0))
    shape = (row_count, col_count, width // row_count, width // col_count)
    return pl.pallas_call(
        product_kernel,
        grid=(depth // tile,),
        in_specs=[spec, spec],
        out_specs=pl.BlockSpec(shape, lambda i: (0, 0, 0, 0)),
        out_shape=jax.ShapeDtypeStruct(shape, jnp.bfloat16),
        scratch_shapes=[pltpu.VMEM((width, width), jnp.float32)],
        compiler_params=pltpu.CompilerParams(vmem_limit_bytes=VMEM_LIMIT),
        cost_estimate=pl.CostEstimate(
            flops=2 * depth * width * width, bytes_accessed=20 * 1024 * 1024, transcendentals=0
        ),
    )(left, right)


def body(generator, listed_block_columns, basis):
    brows, bsize, _ = generator.shape
    states, panel = basis.shape
    reach = brows // 2
    width = reach * bsize
    row_count = lax.axis_size("rows")
    col_count = lax.axis_size("cols")
    up = [(i, i + 1) for i in range(row_count - 1)]
    down = [(j, i) for i, j in up]
    before = lax.ppermute(basis[states - width :], "rows", up)
    after = lax.ppermute(basis[:width], "rows", down)

    first = lax.axis_index("rows") * brows - reach
    index = jnp.where(listed_block_columns >= 0, listed_block_columns - first, brows + 2 * reach).reshape(-1)

    def spread(value):
        parts = value.reshape(col_count, states // col_count, panel)
        return lax.all_to_all(parts, "cols", split_axis=0, concat_axis=0)

    slab_basis = spread(basis)
    applied = apply_blocks(index, before, basis, after, generator)
    slab_applied = spread(applied)
    partial = product(slab_basis, slab_applied, row_count, col_count)
    shares = lax.all_to_all(partial, "rows", split_axis=0, concat_axis=0)
    share = jnp.sum(shares.astype(jnp.float32), axis=0)
    pieces = lax.all_to_all(share, "cols", split_axis=0, concat_axis=0)
    return jnp.sum(pieces, axis=0)


def solution(mesh):
    return jax.shard_map(
        body,
        mesh=mesh,
        in_specs=(P("rows", None, None), P("rows", None), P("rows", "cols")),
        out_specs=P("rows", "cols"),
        check_vma=False,
    )
```

```python
import functools

import jax
import jax.numpy as jnp
from jax import lax
from jax.experimental import pallas as pl
from jax.experimental.pallas import tpu as pltpu
from jax.sharding import PartitionSpec as P

VMEM_LIMIT = 56 * 1024 * 1024


def apply_kernel(index, before, own, after, generator, applied, stacks, sems, *, bsize, slots, group):
    step = pl.program_id(0)
    low, mid = before.shape[0], own.shape[0]
    high = after.shape[0]

    @pl.when(step == 0)
    def _():
        copies = [
            pltpu.make_async_copy(before, stacks.at[pl.ds(0, low)], sems.at[0]),
            pltpu.make_async_copy(own, stacks.at[pl.ds(low, mid)], sems.at[1]),
            pltpu.make_async_copy(after, stacks.at[pl.ds(low + mid, high)], sems.at[2]),
        ]
        for copy in copies:
            copy.start()
        stacks[pl.ds(low + mid + high, bsize), :] = jnp.zeros((bsize, own.shape[1]), own.dtype)
        for copy in copies:
            copy.wait()

    for g in range(group):
        base = (step * group + g) * slots
        blocks = [
            stacks[pl.ds(pl.multiple_of(index[base + s] * bsize, bsize), bsize), :] for s in range(slots)
        ]
        total = jnp.dot(generator[g], jnp.concatenate(blocks, axis=0), preferred_element_type=jnp.float32)
        applied[g * bsize : (g + 1) * bsize, :] = total.astype(applied.dtype)


def apply_blocks(index, before, own, after, generator):
    brows, bsize, width = generator.shape
    slots = width // bsize
    panel = own.shape[1]
    group = 16
    rows = before.shape[0] + own.shape[0] + after.shape[0] + bsize
    anywhere = pl.BlockSpec(memory_space=pl.ANY)
    return pl.pallas_call(
        functools.partial(apply_kernel, bsize=bsize, slots=slots, group=group),
        grid_spec=pltpu.PrefetchScalarGridSpec(
            num_scalar_prefetch=1,
            grid=(brows // group,),
            in_specs=[anywhere, anywhere, anywhere, pl.BlockSpec((group, bsize, width), lambda i, index: (i, 0, 0))],
            out_specs=pl.BlockSpec((group * bsize, panel), lambda i, index: (i, 0)),
            scratch_shapes=[pltpu.VMEM((rows, panel), own.dtype), pltpu.SemaphoreType.DMA((3,))],
        ),
        out_shape=jax.ShapeDtypeStruct(own.shape, own.dtype),
        compiler_params=pltpu.CompilerParams(vmem_limit_bytes=VMEM_LIMIT),
        cost_estimate=pl.CostEstimate(
            flops=2 * brows * bsize * width * panel, bytes_accessed=48 * 1024 * 1024, transcendentals=0
        ),
    )(index, before, own, after, generator)


def product_kernel(left, right, out, total):
    step = pl.program_id(0)
    panels = left.shape[0]

    @pl.when(step == 0)
    def _():
        total[...] = jnp.zeros_like(total)

    rights = jnp.concatenate([right[c] for c in range(right.shape[0])], axis=1)
    panel = left.shape[2]
    for c in range(panels):
        total[c * panel : (c + 1) * panel, :] += lax.dot_general(
            left[c], rights, (((0,), (0,)), ((), ())), preferred_element_type=jnp.float32
        )

    @pl.when(step == pl.num_programs(0) - 1)
    def _():
        height, width = out.shape[2], out.shape[3]
        for r in range(out.shape[0]):
            for c in range(out.shape[1]):
                out[r, c] = total[r * height : (r + 1) * height, c * width : (c + 1) * width].astype(out.dtype)


def product(left, right, row_count, col_count):
    panels, depth, panel = left.shape
    width = panels * panel
    tile = 1024
    spec = pl.BlockSpec((panels, tile, panel), lambda i: (0, i, 0))
    shape = (row_count, col_count, width // row_count, width // col_count)
    return pl.pallas_call(
        product_kernel,
        grid=(depth // tile,),
        in_specs=[spec, spec],
        out_specs=pl.BlockSpec(shape, lambda i: (0, 0, 0, 0)),
        out_shape=jax.ShapeDtypeStruct(shape, jnp.bfloat16),
        scratch_shapes=[pltpu.VMEM((width, width), jnp.float32)],
        compiler_params=pltpu.CompilerParams(vmem_limit_bytes=VMEM_LIMIT),
        cost_estimate=pl.CostEstimate(
            flops=2 * depth * width * width, bytes_accessed=20 * 1024 * 1024, transcendentals=0
        ),
    )(left, right)


def body(generator, listed_block_columns, basis):
    brows, bsize, _ = generator.shape
    states, panel = basis.shape
    reach = brows // 2
    width = reach * bsize
    row_count = lax.axis_size("rows")
    col_count = lax.axis_size("cols")
    up = [(i, i + 1) for i in range(row_count - 1)]
    down = [(j, i) for i, j in up]
    before = lax.ppermute(basis[states - width :], "rows", up)
    after = lax.ppermute(basis[:width], "rows", down)

    first = lax.axis_index("rows") * brows - reach
    index = jnp.where(listed_block_columns >= 0, listed_block_columns - first, brows + 2 * reach).reshape(-1)

    def spread(value):
        parts = value.reshape(col_count, states // col_count, panel)
        return lax.all_to_all(parts, "cols", split_axis=0, concat_axis=0)

    slab_basis = spread(basis)
    applied = apply_blocks(index, before, basis, after, generator)
    slab_applied = spread(applied)
    partial = product(slab_basis, slab_applied, row_count, col_count)
    shares = lax.all_to_all(partial, "rows", split_axis=0, concat_axis=0)
    share = jnp.sum(shares.astype(jnp.float32), axis=0)
    pieces = lax.all_to_all(share, "cols", split_axis=0, concat_axis=0)
    return jnp.sum(pieces, axis=0)


def solution(mesh):
    return jax.shard_map(
        body,
        mesh=mesh,
        in_specs=(P("rows", None, None), P("rows", None), P("rows", "cols")),
        out_specs=P("rows", "cols"),
        check_vma=False,
    )
```

```python
import functools

import jax
import jax.numpy as jnp
from jax import lax
from jax.experimental import pallas as pl
from jax.experimental.pallas import tpu as pltpu
from jax.sharding import PartitionSpec as P

VMEM_LIMIT = 56 * 1024 * 1024


def apply_kernel(index, before, own, after, generator, *rest, bsize, slots, group):
    *parts, stacks, sems = rest
    step = pl.program_id(0)
    low, mid = before.shape[0], own.shape[0]
    high = after.shape[0]

    @pl.when(step == 0)
    def _():
        copies = [
            pltpu.make_async_copy(before, stacks.at[pl.ds(0, low)], sems.at[0]),
            pltpu.make_async_copy(own, stacks.at[pl.ds(low, mid)], sems.at[1]),
            pltpu.make_async_copy(after, stacks.at[pl.ds(low + mid, high)], sems.at[2]),
        ]
        for copy in copies:
            copy.start()
        stacks[pl.ds(low + mid + high, bsize), :] = jnp.zeros((bsize, own.shape[1]), own.dtype)
        for copy in copies:
            copy.wait()

    for g in range(group):
        base = (step * group + g) * slots
        blocks = [
            stacks[pl.ds(pl.multiple_of(index[base + s] * bsize, bsize), bsize), :] for s in range(slots)
        ]
        total = jnp.dot(generator[g], jnp.concatenate(blocks, axis=0), preferred_element_type=jnp.float32)
        width = total.shape[1] // len(parts)
        for p, applied in enumerate(parts):
            applied[g * bsize : (g + 1) * bsize, :] = total[:, p * width : (p + 1) * width].astype(applied.dtype)


def apply_blocks(index, before, own, after, generator, count):
    brows, bsize, width = generator.shape
    slots = width // bsize
    panel = own.shape[1]
    group = 16
    rows = before.shape[0] + own.shape[0] + after.shape[0] + bsize
    anywhere = pl.BlockSpec(memory_space=pl.ANY)
    return pl.pallas_call(
        functools.partial(apply_kernel, bsize=bsize, slots=slots, group=group),
        grid_spec=pltpu.PrefetchScalarGridSpec(
            num_scalar_prefetch=1,
            grid=(brows // group,),
            in_specs=[anywhere, anywhere, anywhere, pl.BlockSpec((group, bsize, width), lambda i, index: (i, 0, 0))],
            out_specs=[pl.BlockSpec((group * bsize, panel // count), lambda i, index: (i, 0))] * count,
            scratch_shapes=[pltpu.VMEM((rows, panel), own.dtype), pltpu.SemaphoreType.DMA((3,))],
        ),
        out_shape=[jax.ShapeDtypeStruct((own.shape[0], panel // count), own.dtype)] * count,
        compiler_params=pltpu.CompilerParams(vmem_limit_bytes=VMEM_LIMIT),
        cost_estimate=pl.CostEstimate(
            flops=2 * brows * bsize * width * panel, bytes_accessed=48 * 1024 * 1024, transcendentals=0
        ),
    )(index, before, own, after, generator)


def product_kernel(left, right, out, total):
    step = pl.program_id(0)
    panels = left.shape[0]

    @pl.when(step == 0)
    def _():
        total[...] = jnp.zeros_like(total)

    rights = jnp.concatenate([right[c] for c in range(right.shape[0])], axis=1)
    panel = left.shape[2]
    for c in range(panels):
        total[c * panel : (c + 1) * panel, :] += lax.dot_general(
            left[c], rights, (((0,), (0,)), ((), ())), preferred_element_type=jnp.float32
        )

    @pl.when(step == pl.num_programs(0) - 1)
    def _():
        height, width = out.shape[2], out.shape[3]
        for r in range(out.shape[0]):
            for c in range(out.shape[1]):
                out[r, c] = total[r * height : (r + 1) * height, c * width : (c + 1) * width].astype(out.dtype)


def product(left, right, row_count, col_count):
    panels, depth, panel = left.shape
    width = panels * panel
    wide = panels * right.shape[2]
    tile = 1024
    specs = [pl.BlockSpec((panels, tile, v.shape[2]), lambda i: (0, i, 0)) for v in (left, right)]
    shape = (row_count, col_count, width // row_count, wide // col_count)
    return pl.pallas_call(
        product_kernel,
        grid=(depth // tile,),
        in_specs=specs,
        out_specs=pl.BlockSpec(shape, lambda i: (0, 0, 0, 0)),
        out_shape=jax.ShapeDtypeStruct(shape, jnp.bfloat16),
        scratch_shapes=[pltpu.VMEM((width, wide), jnp.float32)],
        compiler_params=pltpu.CompilerParams(vmem_limit_bytes=VMEM_LIMIT),
        cost_estimate=pl.CostEstimate(
            flops=2 * depth * width * wide, bytes_accessed=20 * 1024 * 1024, transcendentals=0
        ),
    )(left, right)


def body(generator, listed_block_columns, basis):
    brows, bsize, _ = generator.shape
    states, panel = basis.shape
    reach = brows // 2
    width = reach * bsize
    row_count = lax.axis_size("rows")
    col_count = lax.axis_size("cols")
    up = [(i, i + 1) for i in range(row_count - 1)]
    down = [(j, i) for i, j in up]
    before = lax.ppermute(basis[states - width :], "rows", up)
    after = lax.ppermute(basis[:width], "rows", down)

    first = lax.axis_index("rows") * brows - reach
    index = jnp.where(listed_block_columns >= 0, listed_block_columns - first, brows + 2 * reach).reshape(-1)

    def spread(value):
        parts = value.reshape(col_count, states // col_count, value.shape[1])
        return lax.all_to_all(parts, "cols", split_axis=0, concat_axis=0)

    slab_basis = spread(basis)
    count = max(1, panel // 128)
    results = []
    slabs = []
    held = slab_basis
    for part in apply_blocks(index, before, basis, after, generator, count):
        part, held = lax.optimization_barrier((part, held))
        if not slabs:
            slab_basis = held
        else:
            slabs[-1] = held
        held = spread(part)
        slabs.append(held)
    me = lax.axis_index("rows")
    for p, slab in enumerate(slabs):
        if results:
            slab, results[-1] = lax.optimization_barrier((slab, results[-1]))
        partial = product(slab_basis, slab, row_count, col_count)
        if p + 1 < count:
            mine = lax.dynamic_index_in_dim(partial, me, 0, keepdims=False).astype(jnp.float32)
            for away in range(1, row_count):
                piece = lax.dynamic_index_in_dim(partial, lax.rem(me + away, row_count), 0, keepdims=False)
                pairs = [(i, (i + away) % row_count) for i in range(row_count)]
                mine += lax.ppermute(piece, "rows", pairs).astype(jnp.float32)
        else:
            shares = lax.all_to_all(partial, "rows", split_axis=0, concat_axis=0)
            mine = jnp.sum(shares.astype(jnp.float32), axis=0)
        results.append(mine)
    share = jnp.concatenate(results, axis=2)
    pieces = lax.all_to_all(share, "cols", split_axis=0, concat_axis=0)
    return jnp.sum(pieces, axis=0)


def solution(mesh):
    return jax.shard_map(
        body,
        mesh=mesh,
        in_specs=(P("rows", None, None), P("rows", None), P("rows", "cols")),
        out_specs=P("rows", "cols"),
        check_vma=False,
    )
```

```python
import functools

import jax
import jax.numpy as jnp
from jax import lax
from jax.experimental import pallas as pl
from jax.experimental.pallas import tpu as pltpu
from jax.sharding import PartitionSpec as P

VMEM_LIMIT = 56 * 1024 * 1024


def apply_kernel(index, before, own, after, generator, *rest, bsize, slots, group):
    *parts, stacks, sems = rest
    step = pl.program_id(0)
    low, mid = before.shape[0], own.shape[0]
    high = after.shape[0]

    @pl.when(step == 0)
    def _():
        copies = [
            pltpu.make_async_copy(before, stacks.at[pl.ds(0, low)], sems.at[0]),
            pltpu.make_async_copy(own, stacks.at[pl.ds(low, mid)], sems.at[1]),
            pltpu.make_async_copy(after, stacks.at[pl.ds(low + mid, high)], sems.at[2]),
        ]
        for copy in copies:
            copy.start()
        stacks[pl.ds(low + mid + high, bsize), :] = jnp.zeros((bsize, own.shape[1]), own.dtype)
        for copy in copies:
            copy.wait()

    for g in range(group):
        base = (step * group + g) * slots
        blocks = [
            stacks[pl.ds(pl.multiple_of(index[base + s] * bsize, bsize), bsize), :] for s in range(slots)
        ]
        total = jnp.dot(generator[g], jnp.concatenate(blocks, axis=0), preferred_element_type=jnp.float32)
        width = total.shape[1] // len(parts)
        for p, applied in enumerate(parts):
            applied[g * bsize : (g + 1) * bsize, :] = total[:, p * width : (p + 1) * width].astype(applied.dtype)


def apply_blocks(index, before, own, after, generator, count):
    brows, bsize, width = generator.shape
    slots = width // bsize
    panel = own.shape[1]
    group = 16
    rows = before.shape[0] + own.shape[0] + after.shape[0] + bsize
    anywhere = pl.BlockSpec(memory_space=pl.ANY)
    return pl.pallas_call(
        functools.partial(apply_kernel, bsize=bsize, slots=slots, group=group),
        grid_spec=pltpu.PrefetchScalarGridSpec(
            num_scalar_prefetch=1,
            grid=(brows // group,),
            in_specs=[anywhere, anywhere, anywhere, pl.BlockSpec((group, bsize, width), lambda i, index: (i, 0, 0))],
            out_specs=[pl.BlockSpec((group * bsize, panel // count), lambda i, index: (i, 0))] * count,
            scratch_shapes=[pltpu.VMEM((rows, panel), own.dtype), pltpu.SemaphoreType.DMA((3,))],
        ),
        out_shape=[jax.ShapeDtypeStruct((own.shape[0], panel // count), own.dtype)] * count,
        compiler_params=pltpu.CompilerParams(vmem_limit_bytes=VMEM_LIMIT),
        cost_estimate=pl.CostEstimate(
            flops=2 * brows * bsize * width * panel, bytes_accessed=48 * 1024 * 1024, transcendentals=0
        ),
    )(index, before, own, after, generator)


def product_kernel(left, right, out, total):
    step = pl.program_id(0)
    panels = left.shape[0]

    @pl.when(step == 0)
    def _():
        total[...] = jnp.zeros_like(total)

    rights = jnp.concatenate([right[c] for c in range(right.shape[0])], axis=1)
    panel = left.shape[2]
    for c in range(panels):
        total[c * panel : (c + 1) * panel, :] += lax.dot_general(
            left[c], rights, (((0,), (0,)), ((), ())), preferred_element_type=jnp.float32
        )

    @pl.when(step == pl.num_programs(0) - 1)
    def _():
        height, width = out.shape[2], out.shape[3]
        for r in range(out.shape[0]):
            for c in range(out.shape[1]):
                out[r, c] = total[r * height : (r + 1) * height, c * width : (c + 1) * width].astype(out.dtype)


def product(left, right, row_count, col_count):
    panels, depth, panel = left.shape
    width = panels * panel
    wide = panels * right.shape[2]
    tile = 1024
    specs = [pl.BlockSpec((panels, tile, v.shape[2]), lambda i: (0, i, 0)) for v in (left, right)]
    shape = (row_count, col_count, width // row_count, wide // col_count)
    return pl.pallas_call(
        product_kernel,
        grid=(depth // tile,),
        in_specs=specs,
        out_specs=pl.BlockSpec(shape, lambda i: (0, 0, 0, 0)),
        out_shape=jax.ShapeDtypeStruct(shape, jnp.bfloat16),
        scratch_shapes=[pltpu.VMEM((width, wide), jnp.float32)],
        compiler_params=pltpu.CompilerParams(vmem_limit_bytes=VMEM_LIMIT),
        cost_estimate=pl.CostEstimate(
            flops=2 * depth * width * wide, bytes_accessed=20 * 1024 * 1024, transcendentals=0
        ),
    )(left, right)


def summed(partial, axis):
    shares = lax.all_to_all(partial, axis, split_axis=0, concat_axis=0)
    return jnp.sum(shares.astype(jnp.float32), axis=0)


def summed_by_permutes(partial, axis):
    me, size = lax.axis_index(axis), lax.axis_size(axis)
    mine = lax.dynamic_index_in_dim(partial, me, 0, keepdims=False).astype(jnp.float32)
    for away in range(1, size):
        piece = lax.dynamic_index_in_dim(partial, lax.rem(me + away, size), 0, keepdims=False)
        pairs = [(i, (i + away) % size) for i in range(size)]
        mine += lax.ppermute(piece, axis, pairs).astype(jnp.float32)
    return mine


def body(generator, listed_block_columns, basis):
    brows, bsize, _ = generator.shape
    states, panel = basis.shape
    reach = brows // 2
    width = reach * bsize
    row_count = lax.axis_size("rows")
    col_count = lax.axis_size("cols")
    up = [(i, i + 1) for i in range(row_count - 1)]
    down = [(j, i) for i, j in up]
    before = lax.ppermute(basis[states - width :], "rows", up)
    after = lax.ppermute(basis[:width], "rows", down)

    first = lax.axis_index("rows") * brows - reach
    index = jnp.where(listed_block_columns >= 0, listed_block_columns - first, brows + 2 * reach).reshape(-1)

    def spread(value):
        parts = value.reshape(col_count, states // col_count, value.shape[1])
        return lax.all_to_all(parts, "cols", split_axis=0, concat_axis=0)

    slab_basis = spread(basis)
    count = max(1, panel // 128)
    results = []
    slabs = []
    held = slab_basis
    for part in apply_blocks(index, before, basis, after, generator, count):
        part, held = lax.optimization_barrier((part, held))
        if not slabs:
            slab_basis = held
        else:
            slabs[-1] = held
        held = spread(part)
        slabs.append(held)
    for p, slab in enumerate(slabs):
        if results:
            slab, results[-1] = lax.optimization_barrier((slab, results[-1]))
        partial = product(slab_basis, slab, row_count, col_count)
        for axis in ("rows", "cols"):
            partial = summed_by_permutes(partial, axis) if p + 1 < count else summed(partial, axis)
        results.append(partial)
    return jnp.concatenate(results, axis=1)


def solution(mesh):
    return jax.shard_map(
        body,
        mesh=mesh,
        in_specs=(P("rows", None, None), P("rows", None), P("rows", "cols")),
        out_specs=P("rows", "cols"),
        check_vma=False,
    )
```
